32 devices in a mesh: tm: 8 (over y, x, core), depth: 4 (over z).
Axes of the slice: x: 2, y: 2, z: 4, core: 2. Of those that a mesh axis runs over, the one named last changes fastest.
Arguments:
- basis: bfloat16 [32, 16, 8, 2048], P(None, 'depth', None, 'tm'), may hold values from -0.125 to 0.125
- factors: bfloat16 [512, 32], P('tm'), may hold values from -6 to 6
- measured: bfloat16 [512, 8, 2048], P('tm'), may hold values from 0.29882812 to 3
- shear: int32 [512], P('tm'), may hold values from -3 to 3
- window: int32 [512], P('tm'), may hold values from 0 to 1024
Outputs:
- grad_basis: float32 [32, 16, 8, 2048], P(None, 'depth', None, 'tm')
The draws below stay inside these ranges and needn't reach their ends.
All inputs are finite; a program needn't handle non-finite values.
Results may differ from the reference program's by a relative error of at most 0.0022.
Values may be sent and summed in bfloat16 or wider, within the bound.
A program may use at most 128 MiB of HBM per device.

```python
import math
import jax
import jax.numpy as jnp
from jax import lax

R = 32
W = 2048
H = 8
SHEAR = 3
Z = 16
FRAMES = 512
WD = 1024


def with_ends(drawn, stream_key, least, largest):
    extent = drawn.shape
    spot = [jax.random.randint(jax.random.fold_in(stream_key, axis), (), 0, extent[axis]) for axis in range(len(extent))]
    drawn = drawn.at[tuple(spot)].set(least)
    longest = extent.index(max(extent))
    spot[longest] = (spot[longest] + 1) % extent[longest]
    return drawn.at[tuple(spot)].set(largest)


def steps_of(own_key, shape, cuts, low, top_value):
    def one(axis_at, blocks):
        heights = jax.random.uniform(jax.random.fold_in(jax.random.fold_in(own_key, 6), axis_at), (blocks,), jnp.float32, low / len(cuts), top_value / len(cuts))
        return jnp.repeat(jnp.exp(heights), shape[axis_at] // blocks).reshape((-1,) + (1,) * (len(shape) - axis_at - 1))

    level = one(*cuts[0])
    for cut in cuts[1:]:
        level = level * one(*cut)
    return level


def noise(stream_key, dims, width, bound, cuts=(), held_as=jnp.bfloat16):
    loudness = steps_of(stream_key, dims, cuts, -0.22, 0.18) if cuts else 1.0
    values = jax.random.normal(stream_key, dims, jnp.float32) * width * loudness
    return jnp.minimum(jnp.maximum(values, -bound), bound).astype(held_as)


def setup_inputs(seed: int = 0) -> dict:
    key_list = jax.random.split(jax.random.key(seed), 6)
    basis = noise(key_list[0], (R, Z, H, W), (4 * R * Z) ** -0.5, 0.125, ((1, 4), (3, 8)))
    factors = noise(key_list[1], (FRAMES, R), 1.0, 6.0, ((0, 8),))
    measured = jnp.clip(jnp.exp(math.log(3.0) - 2.306499 * jax.random.uniform(key_list[2], (FRAMES, H, W), jnp.float32) ** steps_of(key_list[2], (FRAMES, H, W), ((0, 8),), -0.2, 0.2)), 0.29882812, 3.0).astype(jnp.bfloat16)
    shear = with_ends(jax.random.randint(key_list[3], (FRAMES,), 0 - SHEAR, SHEAR + 1), jax.random.fold_in(key_list[3], 1), 0 - SHEAR, SHEAR).astype(jnp.int32)
    window = with_ends(jax.random.randint(key_list[4], (FRAMES,), 0, W - WD + 1), jax.random.fold_in(key_list[4], 1), 0, W - WD).astype(jnp.int32)
    return {"basis": basis, "factors": factors, "measured": measured, "shear": shear, "window": window}


def shear_sum(volume, offsets, width_out, margin):
    columns = jnp.arange(width_out, dtype=jnp.int32)
    position = columns[None, None, None, :] + margin + offsets[:, :, None, None]
    position = jnp.broadcast_to(position, volume.shape[:3] + (width_out,))
    return lax.optimization_barrier(jnp.sum(jnp.take_along_axis(volume, position, axis=3), axis=1))

def spread_back(ray_grads, offsets, width_out, margin):
    shape_full = (ray_grads.shape[0], offsets.shape[1], ray_grads.shape[1], ray_grads.shape[2])
    widened = jnp.broadcast_to(ray_grads[:, None], shape_full)
    columns = jnp.arange(width_out, dtype=jnp.int32)
    position = columns[None, None, None, :] + margin - offsets[:, :, None, None]
    position = jnp.broadcast_to(position, shape_full[:3] + (width_out,))
    return jnp.take_along_axis(widened, position, axis=3)

def reference(basis, factors, measured, shear, window):
    margin = SHEAR * (Z // 2)
    depth_ids = jnp.arange(Z, dtype=jnp.int32) - Z // 2
    offsets = (shear[:, None] * depth_ids[None, :]).astype(jnp.int32)
    widened = jnp.pad(basis, ((0, 0), (0, 0), (0, 0), (margin, margin)))
    block_rows = 32 if FRAMES % 32 == 0 else FRAMES
    block_count = FRAMES // block_rows
    factor_blocks = factors.reshape(block_count, block_rows, R)
    offset_blocks = offsets.reshape(block_count, block_rows, Z)

    def forward_block(pieces):
        factor_block, offset_block = pieces
        volume = jnp.einsum('tr,rzhw->tzhw', factor_block.astype(jnp.float32), widened.astype(jnp.float32))
        return shear_sum(volume, offset_block, W, margin)
    projection = lax.map(forward_block, (factor_blocks, offset_blocks)).reshape(FRAMES, H, W)
    transmit = jnp.exp(-projection)
    columns = jnp.arange(W, dtype=jnp.int32)
    inside = (columns[None, None, :] >= window[:, None, None]) & (columns[None, None, :] < window[:, None, None] + WD)
    residual = jnp.where(inside, transmit - measured.astype(jnp.float32), jnp.float32(0.0))
    norm_scale = 1.0 / math.sqrt(FRAMES)
    ray_grad = (-transmit * residual * norm_scale).astype(jnp.bfloat16)
    grad_blocks = ray_grad.reshape(block_count, block_rows, H, W)

    def backward_block(running, pieces):
        factor_block, offset_block, grad_block = pieces
        spread = spread_back(jnp.pad(grad_block, ((0, 0), (0, 0), (margin, margin))), offset_block, W, margin)
        return (running + jnp.einsum('tr,tzhw->rzhw', factor_block.astype(jnp.float32), spread.astype(jnp.float32)), None)
    start_value = jnp.zeros((R, Z, H, W), jnp.float32)
    result, _ = lax.scan(backward_block, start_value, (factor_blocks, offset_blocks, grad_blocks))
    return result
```

```python
import functools
import math

import jax
import jax.numpy as jnp
from jax import lax
from jax.experimental import pallas as pl
from jax.experimental.pallas import tpu as pltpu
from jax.sharding import PartitionSpec as P

SHEAR = 3
WD = 1024
LANES = 128
STEPS = 2 * SHEAR + 1


def kernel(
    dims,
    main_ref,
    halo_ref,
    meas_ref,
    out_ref,
    in_main,
    in_halo,
    in_meas,
    back_main,
    back_spill,
    got_main,
    got_spill,
    coef,
    sheared,
    proj,
    grad,
    spread,
    send_main,
    recv_main,
    send_halo,
    recv_halo,
    send_meas,
    recv_meas,
    send_out,
    recv_out,
    send_spill,
    recv_spill,
):
    T, D, LD, HS, C, R, HL, FB = dims
    N = HS * C
    WIDE = C + LANES
    per = LANES // HL
    half = LD * D // 2
    me = lax.axis_index("tm")
    dep = lax.axis_index("depth")
    left = lax.rem(me + T - 1, T)
    right = lax.rem(me + 1, T)

    def peer(base, k, n):
        return lax.rem(base + k, n)

    def at(tm, depth):
        return {"tm": tm, "depth": depth}

    def remote(src, dst, send, recv, where):
        return pltpu.make_async_remote_copy(
            src_ref=src,
            dst_ref=dst,
            send_sem=send,
            recv_sem=recv,
            device_id=where,
            device_id_type=pl.DeviceIdType.MESH,
        )

    barrier = pltpu.get_barrier_semaphore()
    greeted = 0
    for k in range(1, T):
        pl.semaphore_signal(
            barrier, inc=1, device_id=at(peer(me, k, T), dep), device_id_type=pl.DeviceIdType.MESH
        )
        greeted += 1
    for k in range(1, D):
        for tm in (me, left, right):
            pl.semaphore_signal(
                barrier, inc=1, device_id=at(tm, peer(dep, k, D)), device_id_type=pl.DeviceIdType.MESH
            )
            greeted += 1
    in_main[dep] = main_ref[dep]
    in_meas[me] = meas_ref[me]
    pl.semaphore_wait(barrier, greeted)

    def main_copy(k):
        to = peer(dep, k, D)
        return remote(main_ref.at[to], in_main.at[dep], send_main.at[k], recv_main.at[dep], at(me, to))

    def halo_copy(side, k):
        to = peer(dep, k, D)
        return remote(
            halo_ref.at[side, to],
            in_halo.at[side, dep],
            send_halo.at[side, k],
            recv_halo.at[side, dep],
            at((left, right)[side], to),
        )

    def meas_copy(k):
        to = peer(me, k, T)
        return remote(meas_ref.at[to], in_meas.at[me], send_meas.at[k], recv_meas.at[me], at(to, dep))

    sends = []
    for k in list(range(1, D)) + [0]:
        if k:
            sends.append(main_copy(k))
        for side in (0, 1):
            sends.append(halo_copy(side, k))
    for k in range(1, T):
        sends.append(meas_copy(k))
    for copy in sends:
        copy.start()

    for k in range(1, T):
        source = peer(me, k, T)
        remote(
            meas_ref.at[source], in_meas.at[source], send_meas.at[k], recv_meas.at[source], at(source, dep)
        ).wait_recv()

    lane = lax.broadcasted_iota(jnp.int32, (FB, LANES), 1)
    group = (lane // R).astype(jnp.float32)

    def coef_step(j, carry):
        info = in_meas[j, :, N:].astype(jnp.float32)
        first = jnp.where(lane < R, info, 0.0)
        tiled = first
        for q in range(1, LANES // R):
            tiled = tiled + pltpu.roll(first, q * R, 1)
        step = info[:, R : R + 1] + float(SHEAR)
        rows = pl.ds(pl.multiple_of(j * FB, FB), FB)
        for b in range(2):
            coef[rows, b * LANES : (b + 1) * LANES] = jnp.where(
                step == group + float(b * (LANES // R)), tiled, 0.0
            ).astype(jnp.bfloat16)
        return carry

    lax.fori_loop(0, T, coef_step, 0)

    edge = lax.broadcasted_iota(jnp.int32, (R, LANES), 1)
    has_right = me < T - 1
    has_left = me > 0

    sheared[...] = jnp.zeros_like(sheared)
    for q in range(D):

        @pl.when(q != dep)
        def _():
            remote(main_ref.at[q], in_main.at[q], send_main.at[0], recv_main.at[q], at(me, q)).wait_recv()

        for side in (0, 1):
            remote(
                halo_ref.at[side, q],
                in_halo.at[side, q],
                send_halo.at[side, 0],
                recv_halo.at[side, q],
                at((right, left)[side], q),
            ).wait_recv()

        def shear_step(h, carry):
            columns = pl.ds(pl.multiple_of(h * C, LANES), C)
            wides = []
            for l in range(LD):
                g, p = divmod(l, per)
                body = in_main[q, h, l * R : (l + 1) * R, :].astype(jnp.float32)
                after = in_halo[0, q, h, g * R : (g + 1) * R, :].astype(jnp.float32)
                before = in_halo[1, q, h, g * R : (g + 1) * R, :].astype(jnp.float32)
                after = pltpu.roll(after, (LANES - p * HL) % LANES, 1)
                before = pltpu.roll(before, (2 * LANES - HL - p * HL) % LANES, 1)
                rim = jnp.where(
                    jnp.logical_and(edge < HL, has_right),
                    after,
                    jnp.where(jnp.logical_and(edge >= LANES - HL, has_left), before, 0.0),
                )
                wides.append(jnp.concatenate([body, rim], axis=1))
            for s in range(STEPS):
                total = sheared[s * R : (s + 1) * R, columns]
                for l in range(LD):
                    shift = (s - SHEAR) * (q * LD + l - half)
                    turned = pltpu.roll(wides[l], (-shift) % WIDE, 1) if shift else wides[l]
                    total = total + turned[:, :C]
                sheared[s * R : (s + 1) * R, columns] = total
            return carry

        lax.fori_loop(0, HS, shear_step, 0)

    table = sheared[...]
    high = table.astype(jnp.bfloat16)
    low = (table - high.astype(jnp.float32)).astype(jnp.bfloat16)
    proj[...] = jnp.dot(coef[...], high, preferred_element_type=jnp.float32) + jnp.dot(
        coef[...], low, preferred_element_type=jnp.float32
    )

    norm_scale = 1.0 / math.sqrt(T * FB)
    column = lax.broadcasted_iota(jnp.int32, (FB, N), 1)
    column = (lax.rem(column, C) + me * C).astype(jnp.float32)

    def ray_step(j, carry):
        rows = pl.ds(pl.multiple_of(j * FB, FB), FB)
        info = in_meas[j, :, N:].astype(jnp.float32)
        start = info[:, R + 1 : R + 2] + info[:, R + 2 : R + 3]
        transmit = jnp.exp(-proj[rows, :])
        inside = jnp.logical_and(column >= start, column < start + float(WD))
        residual = jnp.where(inside, transmit - in_meas[j, :, :N].astype(jnp.float32), 0.0)
        grad[rows, :] = (-transmit * residual * norm_scale).astype(jnp.bfloat16)
        return carry

    lax.fori_loop(0, T, ray_step, 0)

    spread[...] = lax.dot_general(
        coef[...], grad[...], (((0,), (0,)), ((), ())), preferred_element_type=jnp.float32
    )

    blank = jnp.zeros((R, LANES), jnp.float32)

    def spill_copy(side, q):
        return remote(
            back_spill.at[side, q],
            got_spill.at[side, dep],
            send_spill.at[side, q],
            recv_spill.at[side, dep],
            at((right, left)[side], q),
        )

    def back_copy(q):
        return remote(back_main.at[q], got_main.at[dep], send_out.at[q], recv_out.at[dep], at(me, q))

    for q in range(D):

        def back_step(h, carry):
            columns = pl.ds(pl.multiple_of(h * C, LANES), C)
            totals = [None] * LD
            for s in range(STEPS):
                piece = jnp.concatenate([spread[s * R : (s + 1) * R, columns], blank], axis=1)
                for l in range(LD):
                    shift = (s - SHEAR) * (q * LD + l - half)
                    turned = pltpu.roll(piece, shift % WIDE, 1) if shift else piece
                    totals[l] = turned if s == 0 else totals[l] + turned
            for g in range(LD // per):
                ahead = blank
                behind = blank
                for p in range(per):
                    rim = totals[g * per + p][:, C:]
                    fore = jnp.where(edge < HL, rim, 0.0)
                    aft = jnp.where(edge >= LANES - HL, rim, 0.0)
                    ahead = ahead + (pltpu.roll(fore, p * HL, 1) if p else fore)
                    turn = (p * HL + HL) % LANES
                    behind = behind + (pltpu.roll(aft, turn, 1) if turn else aft)
                back_spill[0, q, h, g * R : (g + 1) * R, :] = ahead.astype(jnp.bfloat16)
                back_spill[1, q, h, g * R : (g + 1) * R, :] = behind.astype(jnp.bfloat16)
            for l in range(LD):
                back_main[q, h, l * R : (l + 1) * R, :] = totals[l][:, :C].astype(jnp.bfloat16)

            @pl.when(q == dep)
            def _():
                for l in range(LD):
                    out_ref[dep * HS + h, l * R : (l + 1) * R, :] = totals[l][:, :C]

            return carry

        lax.fori_loop(0, HS, back_step, 0)

        @pl.when(q != dep)
        def _():
            back_copy(q).start()

        for side in (0, 1):
            spill_copy(side, q).start()

    for k in range(D):
        source = peer(dep, k, D)
        if k:
            remote(
                back_main.at[source], got_main.at[source], send_out.at[0], recv_out.at[source], at(me, source)
            ).wait_recv()
        for side in (0, 1):
            remote(
                back_spill.at[side, source],
                got_spill.at[side, source],
                send_spill.at[side, 0],
                recv_spill.at[side, source],
                at((left, right)[side], source),
            ).wait_recv()

        def gather_step(h, carry):
            for l in range(LD):
                g, p = divmod(l, per)
                rows = slice(l * R, (l + 1) * R)
                if k:
                    total = got_main[source, h, rows, :].astype(jnp.float32)
                else:
                    total = out_ref[source * HS + h, rows, :]
                fore = got_spill[0, source, h, g * R : (g + 1) * R, :].astype(jnp.float32)
                aft = got_spill[1, source, h, g * R : (g + 1) * R, :].astype(jnp.float32)
                fore = pltpu.roll(fore, (LANES - p * HL) % LANES, 1)
                aft = pltpu.roll(aft, (2 * LANES - HL - p * HL) % LANES, 1)
                fore = jnp.where(jnp.logical_and(edge < HL, has_left), fore, 0.0)
                aft = jnp.where(jnp.logical_and(edge >= LANES - HL, has_right), aft, 0.0)
                blocks = [total[:, b : b + LANES] for b in range(0, C, LANES)]
                blocks[0] = blocks[0] + fore
                blocks[-1] = blocks[-1] + aft
                for b, block in enumerate(blocks):
                    out_ref[source * HS + h, rows, b * LANES : (b + 1) * LANES] = block
            return carry

        lax.fori_loop(0, HS, gather_step, 0)

    for copy in sends:
        copy.wait_send()
    for q in range(D):

        @pl.when(q != dep)
        def _():
            back_copy(q).wait_send()

        for side in (0, 1):
            spill_copy(side, q).wait_send()


def per_device(basis, factors, measured, shear, window):
    R, LD, H, C = basis.shape
    FB, W = factors.shape[0], measured.shape[2]
    T, D = lax.axis_size("tm"), lax.axis_size("depth")
    HS = H // D
    N = HS * C
    HL = 32
    while HL < SHEAR * (LD * D // 2):
        HL *= 2
    per = LANES // HL
    G = LD // per

    rows = jnp.transpose(basis, (2, 1, 0, 3)).reshape(D, HS, LD * R, C)

    def pack(columns):
        parts = columns.reshape(D, HS, G, per, R, HL)
        return jnp.transpose(parts, (0, 1, 2, 4, 3, 5)).reshape(D, HS, G * R, LANES)

    halo = jnp.stack([pack(rows[..., :HL]), pack(rows[..., C - HL :])])

    mine = lax.dynamic_slice_in_dim(measured, lax.axis_index("depth") * HS, HS, 1)
    mine = jnp.transpose(mine.reshape(FB, HS, T, C), (2, 0, 1, 3)).reshape(T, FB, N)
    low = window % 32
    facts = jnp.concatenate(
        [
            factors,
            jnp.stack([shear, window - low, low], 1).astype(jnp.bfloat16),
            jnp.zeros((FB, LANES - R - 3), jnp.bfloat16),
        ],
        1,
    )
    mine = jnp.concatenate([mine, jnp.broadcast_to(facts[None], (T, FB, LANES))], 2)

    bf, f32 = jnp.bfloat16, jnp.float32
    dma = pltpu.SemaphoreType.DMA
    out = pl.pallas_call(
        functools.partial(kernel, (T, D, LD, HS, C, R, HL, FB)),
        out_shape=jax.ShapeDtypeStruct((H, LD * R, C), f32),
        in_specs=[pl.BlockSpec(memory_space=pltpu.VMEM)] * 3,
        out_specs=pl.BlockSpec(memory_space=pltpu.VMEM),
        scratch_shapes=[
            pltpu.VMEM((D, HS, LD * R, C), bf),
            pltpu.VMEM((2, D, HS, G * R, LANES), bf),
            pltpu.VMEM((T, FB, N + LANES), bf),
            pltpu.VMEM((D, HS, LD * R, C), bf),
            pltpu.VMEM((2, D, HS, G * R, LANES), bf),
            pltpu.VMEM((D, HS, LD * R, C), bf),
            pltpu.VMEM((2, D, HS, G * R, LANES), bf),
            pltpu.VMEM((T * FB, 2 * LANES), bf),
            pltpu.VMEM((2 * LANES, N), f32),
            pltpu.VMEM((T * FB, N), f32),
            pltpu.VMEM((T * FB, N), bf),
            pltpu.VMEM((2 * LANES, N), f32),
            dma((D,)),
            dma((D,)),
            dma((2, D)),
            dma((2, D)),
            dma((T,)),
            dma((T,)),
            dma((D,)),
            dma((D,)),
            dma((2, D)),
            dma((2, D)),
        ],
        compiler_params=pltpu.CompilerParams(
            collective_id=0, has_side_effects=True, vmem_limit_bytes=40 * 1024 * 1024
        ),
    )(rows, halo, mine)
    return jnp.transpose(out.reshape(H, LD, R, C), (2, 1, 0, 3))


def solution(mesh):
    in_specs = (P(None, "depth", None, "tm"), P("tm", None), P("tm", None, None), P("tm"), P("tm"))
    out_specs = P(None, "depth", None, "tm")
    return jax.shard_map(
        per_device, mesh=mesh, in_specs=in_specs, out_specs=out_specs, check_vma=False
    )
```

```python
import functools
import math

import jax
import jax.numpy as jnp
from jax import lax
from jax.experimental import pallas as pl
from jax.experimental.pallas import tpu as pltpu
from jax.sharding import PartitionSpec as P

SHEAR = 3
WD = 1024
LANES = 128
STEPS = 2 * SHEAR + 1


def kernel(
    dims,
    main_ref,
    fact_ref,
    shear_ref,
    window_ref,
    meas_ref,
    out_ref,
    meas_all,
    snd_halo,
    snd_meas,
    in_main,
    in_halo,
    in_meas,
    back_main,
    back_spill,
    got_main,
    got_spill,
    coef,
    sheared,
    proj,
    grad,
    spread,
    load_sem,
    send_main,
    recv_main,
    send_halo,
    recv_halo,
    send_meas,
    recv_meas,
    send_out,
    recv_out,
    send_spill,
    recv_spill,
):
    T, D, LD, HS, C, R, HL, FB, H = dims
    N = HS * C
    WIDE = C + LANES
    per = LANES // HL
    G = LD // per
    half = LD * D // 2
    me = lax.axis_index("tm")
    dep = lax.axis_index("depth")
    left = lax.rem(me + T - 1, T)
    right = lax.rem(me + 1, T)
    outward = []
    for q in range((D + 1) // 2):
        outward += [q] if q == D - 1 - q else [q, D - 1 - q]

    def peer(base, k, n):
        return lax.rem(base + k, n)

    def at(tm, depth):
        return {"tm": tm, "depth": depth}

    def remote(src, dst, send, recv, where):
        return pltpu.make_async_remote_copy(
            src_ref=src,
            dst_ref=dst,
            send_sem=send,
            recv_sem=recv,
            device_id=where,
            device_id_type=pl.DeviceIdType.MESH,
        )

    load = pltpu.make_async_copy(meas_ref, meas_all, load_sem)
    load.start()

    barrier = pltpu.get_barrier_semaphore()
    greeted = 0
    for k in range(1, T):
        pl.semaphore_signal(
            barrier, inc=1, device_id=at(peer(me, k, T), dep), device_id_type=pl.DeviceIdType.MESH
        )
        greeted += 1
    for k in range(1, D):
        for tm in (me, left, right):
            pl.semaphore_signal(
                barrier, inc=1, device_id=at(tm, peer(dep, k, D)), device_id_type=pl.DeviceIdType.MESH
            )
            greeted += 1

    edge = lax.broadcasted_iota(jnp.int32, (R, LANES), 1)
    has_right = me < T - 1
    has_left = me > 0
    blank = jnp.zeros((R, LANES), jnp.float32)

    def pack(blocks_low, blocks_high):
        low = blank
        high = blank
        for p in range(per):
            fore = jnp.where(edge < HL, blocks_low[p], 0.0)
            aft = jnp.where(edge >= LANES - HL, blocks_high[p], 0.0)
            low = low + (pltpu.roll(fore, p * HL, 1) if p else fore)
            turn = (p * HL + HL) % LANES
            high = high + (pltpu.roll(aft, turn, 1) if turn else aft)
        return low.astype(jnp.bfloat16), high.astype(jnp.bfloat16)

    def pack_step(n, carry):
        q = n // HS
        h = n % HS
        for g in range(G):
            heads = []
            tails = []
            for p in range(per):
                rows = slice((g * per + p) * R, (g * per + p + 1) * R)
                heads.append(main_ref[q, h, rows, :LANES].astype(jnp.float32))
                tails.append(main_ref[q, h, rows, C - LANES :].astype(jnp.float32))
            low, high = pack(heads, tails)
            snd_halo[0, q, h, g * R : (g + 1) * R, :] = low
            snd_halo[1, q, h, g * R : (g + 1) * R, :] = high
        return carry

    lax.fori_loop(0, D * HS, pack_step, 0)
    in_main[dep] = main_ref[dep]
    pl.semaphore_wait(barrier, greeted)

    def main_copy(k, h):
        to = peer(dep, k, D)
        return remote(
            main_ref.at[to, h], in_main.at[dep, h], send_main.at[k, h], recv_main.at[dep, h], at(me, to)
        )

    def halo_copy(side, k, h):
        to = peer(dep, k, D)
        return remote(
            snd_halo.at[side, to, h],
            in_halo.at[side, dep, h],
            send_halo.at[side, k, h],
            recv_halo.at[side, dep, h],
            at((left, right)[side], to),
        )

    def meas_copy(k):
        to = peer(me, k, T)
        return remote(snd_meas.at[to], in_meas.at[me], send_meas.at[k], recv_meas.at[me], at(to, dep))

    def send_step(h, carry):
        for k in list(range(1, D)) + [0]:
            if k:
                main_copy(k, h).start()
            for side in (0, 1):
                halo_copy(side, k, h).start()
        return carry

    lax.fori_loop(0, HS, send_step, 0)

    row = lax.broadcasted_iota(jnp.int32, (FB, FB), 0)
    diagonal = row == lax.broadcasted_iota(jnp.int32, (FB, FB), 1)

    def upright(values):
        spread_out = jnp.broadcast_to(values.astype(jnp.float32), (FB, FB))
        return jnp.sum(jnp.where(diagonal, spread_out, 0.0), axis=1, keepdims=True)

    low_bits = window_ref[...] & 31
    lane = lax.broadcasted_iota(jnp.int32, (FB, LANES), 1)
    pick = lax.broadcasted_iota(jnp.int32, (R, LANES), 0) == edge
    pick = jnp.where(pick, 1.0, 0.0).astype(jnp.bfloat16)
    facts = lax.dot_general(
        fact_ref[...], pick, (((0,), (0,)), ((), ())), preferred_element_type=jnp.float32
    )
    facts = jnp.where(lane == R, upright(shear_ref[...]), facts)
    facts = jnp.where(lane == R + 1, upright(window_ref[...] - low_bits), facts)
    facts = jnp.where(lane == R + 2, upright(low_bits), facts)
    facts = facts.astype(jnp.bfloat16)

    wanted = lax.broadcasted_iota(jnp.int32, (HS * FB, FB * H), 0)
    wanted = lax.rem(wanted, FB) * H + dep * HS + lax.div(wanted, FB)
    select = wanted == lax.broadcasted_iota(jnp.int32, (HS * FB, FB * H), 1)
    select = jnp.where(select, 1.0, 0.0).astype(jnp.bfloat16)
    load.wait()
    for j in range(T):
        picked = jnp.dot(
            select, meas_all[:, j * C : (j + 1) * C], preferred_element_type=jnp.float32
        ).astype(jnp.bfloat16)
        for h in range(HS):
            snd_meas[j, :, h * C : (h + 1) * C] = picked[h * FB : (h + 1) * FB, :]
        snd_meas[j, :, N:] = facts

    for k in range(1, T):
        meas_copy(k).start()
    in_meas[me] = snd_meas[me]
    for k in range(1, T):
        source = peer(me, k, T)
        remote(
            snd_meas.at[source], in_meas.at[source], send_meas.at[k], recv_meas.at[source], at(source, dep)
        ).wait_recv()

    group = (lane // R).astype(jnp.float32)

    def coef_step(j, carry):
        info = in_meas[j, :, N:].astype(jnp.float32)
        first = jnp.where(lane < R, info, 0.0)
        tiled = first
        for q in range(1, LANES // R):
            tiled = tiled + pltpu.roll(first, q * R, 1)
        step = info[:, R : R + 1] + float(SHEAR)
        rows = pl.ds(pl.multiple_of(j * FB, FB), FB)
        for b in range(2):
            coef[rows, b * LANES : (b + 1) * LANES] = jnp.where(
                step == group + float(b * (LANES // R)), tiled, 0.0
            ).astype(jnp.bfloat16)
        return carry

    lax.fori_loop(0, T, coef_step, 0)

    norm_scale = 1.0 / math.sqrt(T * FB)
    column = lax.broadcasted_iota(jnp.int32, (FB, C), 1) + me * C
    column = column.astype(jnp.float32)

    def back_copy(q, h):
        return remote(
            back_main.at[q, h], got_main.at[dep, h], send_out.at[q, h], recv_out.at[dep, h], at(me, q)
        )

    def spill_copy(side, q, h):
        return remote(
            back_spill.at[side, q, h],
            got_spill.at[side, dep, h],
            send_spill.at[side, q, h],
            recv_spill.at[side, dep, h],
            at((right, left)[side], q),
        )

    def row_step(h, carry):
        columns = pl.ds(pl.multiple_of(h * C, LANES), C)
        sheared[...] = jnp.zeros_like(sheared)
        for q in outward[::-1]:

            @pl.when(q != dep)
            def _():
                remote(
                    main_ref.at[q, h], in_main.at[q, h], send_main.at[0, h], recv_main.at[q, h], at(me, q)
                ).wait_recv()

            for side in (0, 1):
                remote(
                    snd_halo.at[side, q, h],
                    in_halo.at[side, q, h],
                    send_halo.at[side, 0, h],
                    recv_halo.at[side, q, h],
                    at((right, left)[side], q),
                ).wait_recv()
            wides = []
            for l in range(LD):
                g, p = divmod(l, per)
                body = in_main[q, h, l * R : (l + 1) * R, :].astype(jnp.float32)
                after = in_halo[0, q, h, g * R : (g + 1) * R, :].astype(jnp.float32)
                before = in_halo[1, q, h, g * R : (g + 1) * R, :].astype(jnp.float32)
                after = pltpu.roll(after, (LANES - p * HL) % LANES, 1)
                before = pltpu.roll(before, (2 * LANES - HL - p * HL) % LANES, 1)
                rim = jnp.where(
                    jnp.logical_and(edge < HL, has_right),
                    after,
                    jnp.where(jnp.logical_and(edge >= LANES - HL, has_left), before, 0.0),
                )
                wides.append(jnp.concatenate([body, rim], axis=1))
            for s in range(STEPS):
                total = sheared[s * R : (s + 1) * R, :]
                for l in range(LD):
                    shift = (s - SHEAR) * (q * LD + l - half)
                    turned = pltpu.roll(wides[l], (-shift) % WIDE, 1) if shift else wides[l]
                    total = total + turned[:, :C]
                sheared[s * R : (s + 1) * R, :] = total

        table = sheared[...]
        high = table.astype(jnp.bfloat16)
        low = (table - high.astype(jnp.float32)).astype(jnp.bfloat16)
        proj[...] = jnp.dot(coef[...], high, preferred_element_type=jnp.float32) + jnp.dot(
            coef[...], low, preferred_element_type=jnp.float32
        )

        def ray_step(j, carry):
            rows = pl.ds(pl.multiple_of(j * FB, FB), FB)
            info = in_meas[j, :, N:].astype(jnp.float32)
            start = info[:, R + 1 : R + 2] + info[:, R + 2 : R + 3]
            transmit = jnp.exp(-proj[rows, :])
            inside = jnp.logical_and(column >= start, column < start + float(WD))
            residual = jnp.where(inside, transmit - in_meas[j, :, columns].astype(jnp.float32), 0.0)
            grad[rows, :] = (-transmit * residual * norm_scale).astype(jnp.bfloat16)
            return carry

        lax.fori_loop(0, T, ray_step, 0)
        spread[...] = lax.dot_general(
            coef[...], grad[...], (((0,), (0,)), ((), ())), preferred_element_type=jnp.float32
        )

        for q in outward:
            totals = [None] * LD
            for s in range(STEPS):
                piece = jnp.concatenate([spread[s * R : (s + 1) * R, :], blank], axis=1)
                for l in range(LD):
                    shift = (s - SHEAR) * (q * LD + l - half)
                    turned = pltpu.roll(piece, shift % WIDE, 1) if shift else piece
                    totals[l] = turned if s == 0 else totals[l] + turned
            for l in range(LD):
                back_main[q, h, l * R : (l + 1) * R, :] = totals[l][:, :C].astype(jnp.bfloat16)

            @pl.when(q == dep)
            def _():
                for l in range(LD):
                    out_ref[dep * HS + h, l * R : (l + 1) * R, :] = totals[l][:, :C]

            @pl.when(q != dep)
            def _():
                back_copy(q, h).start()

            for g in range(G):
                rims = [totals[g * per + p][:, C:] for p in range(per)]
                ahead, behind = pack(rims, rims)
                back_spill[0, q, h, g * R : (g + 1) * R, :] = ahead
                back_spill[1, q, h, g * R : (g + 1) * R, :] = behind
            for side in (0, 1):
                spill_copy(side, q, h).start()
        return carry

    lax.fori_loop(0, HS, row_step, 0)

    def gather_step(h, carry):
        for k in range(D):
            source = peer(dep, k, D)
            if k:
                remote(
                    back_main.at[source, h],
                    got_main.at[source, h],
                    send_out.at[0, h],
                    recv_out.at[source, h],
                    at(me, source),
                ).wait_recv()
            for side in (0, 1):
                remote(
                    back_spill.at[side, source, h],
                    got_spill.at[side, source, h],
                    send_spill.at[side, 0, h],
                    recv_spill.at[side, source, h],
                    at((left, right)[side], source),
                ).wait_recv()
            for l in range(LD):
                g, p = divmod(l, per)
                rows = slice(l * R, (l + 1) * R)
                if k:
                    total = got_main[source, h, rows, :].astype(jnp.float32)
                else:
                    total = out_ref[source * HS + h, rows, :]
                fore = got_spill[0, source, h, g * R : (g + 1) * R, :].astype(jnp.float32)
                aft = got_spill[1, source, h, g * R : (g + 1) * R, :].astype(jnp.float32)
                fore = pltpu.roll(fore, (LANES - p * HL) % LANES, 1)
                aft = pltpu.roll(aft, (2 * LANES - HL - p * HL) % LANES, 1)
                fore = jnp.where(jnp.logical_and(edge < HL, has_left), fore, 0.0)
                aft = jnp.where(jnp.logical_and(edge >= LANES - HL, has_right), aft, 0.0)
                blocks = [total[:, b : b + LANES] for b in range(0, C, LANES)]
                blocks[0] = blocks[0] + fore
                blocks[-1] = blocks[-1] + aft
                for b, block in enumerate(blocks):
                    out_ref[source * HS + h, rows, b * LANES : (b + 1) * LANES] = block
        return carry

    lax.fori_loop(0, HS, gather_step, 0)

    for k in range(1, T):
        meas_copy(k).wait_send()

    def drain_step(h, carry):
        for k in range(D):
            if k:
                main_copy(k, h).wait_send()
            for side in (0, 1):
                halo_copy(side, k, h).wait_send()
        for q in range(D):

            @pl.when(q != dep)
            def _():
                back_copy(q, h).wait_send()

            for side in (0, 1):
                spill_copy(side, q, h).wait_send()
        return carry

    lax.fori_loop(0, HS, drain_step, 0)


def per_device(basis, factors, measured, shear, window):
    R, LD, H, C = basis.shape
    FB, W = factors.shape[0], measured.shape[2]
    T, D = lax.axis_size("tm"), lax.axis_size("depth")
    HS = H // D
    N = HS * C
    HL = 32
    while HL < SHEAR * (LD * D // 2):
        HL *= 2
    G = LD // (LANES // HL)

    rows = jnp.transpose(basis, (2, 1, 0, 3)).reshape(D, HS, LD * R, C)

    bf, f32 = jnp.bfloat16, jnp.float32
    dma = pltpu.SemaphoreType.DMA
    whole = pl.BlockSpec(memory_space=pltpu.VMEM)
    out = pl.pallas_call(
        functools.partial(kernel, (T, D, LD, HS, C, R, HL, FB, H)),
        out_shape=jax.ShapeDtypeStruct((H, LD * R, C), f32),
        in_specs=[whole, whole, whole, whole, pl.BlockSpec(memory_space=pl.ANY)],
        out_specs=whole,
        scratch_shapes=[
            pltpu.VMEM((FB * H, W), bf),
            pltpu.VMEM((2, D, HS, G * R, LANES), bf),
            pltpu.VMEM((T, FB, N + LANES), bf),
            pltpu.VMEM((D, HS, LD * R, C), bf),
            pltpu.VMEM((2, D, HS, G * R, LANES), bf),
            pltpu.VMEM((T, FB, N + LANES), bf),
            pltpu.VMEM((D, HS, LD * R, C), bf),
            pltpu.VMEM((2, D, HS, G * R, LANES), bf),
            pltpu.VMEM((D, HS, LD * R, C), bf),
            pltpu.VMEM((2, D, HS, G * R, LANES), bf),
            pltpu.VMEM((T * FB, 2 * LANES), bf),
            pltpu.VMEM((2 * LANES, C), f32),
            pltpu.VMEM((T * FB, C), f32),
            pltpu.VMEM((T * FB, C), bf),
            pltpu.VMEM((2 * LANES, C), f32),
            dma,
            dma((D, HS)),
            dma((D, HS)),
            dma((2, D, HS)),
            dma((2, D, HS)),
            dma((T,)),
            dma((T,)),
            dma((D, HS)),
            dma((D, HS)),
            dma((2, D, HS)),
            dma((2, D, HS)),
        ],
        compiler_params=pltpu.CompilerParams(
            collective_id=0, has_side_effects=True, vmem_limit_bytes=60 * 1024 * 1024
        ),
    )(rows, factors.T, shear.reshape(1, FB), window.reshape(1, FB), measured.reshape(FB * H, W))
    return jnp.transpose(out.reshape(H, LD, R, C), (2, 1, 0, 3))


def solution(mesh):
    in_specs = (P(None, "depth", None, "tm"), P("tm", None), P("tm", None, None), P("tm"), P("tm"))
    out_specs = P(None, "depth", None, "tm")
    return jax.shard_map(
        per_device, mesh=mesh, in_specs=in_specs, out_specs=out_specs, check_vma=False
    )
```

```python
import functools
import math

import jax
import jax.numpy as jnp
from jax import lax
from jax.experimental import pallas as pl
from jax.experimental.pallas import tpu as pltpu
from jax.sharding import PartitionSpec as P

SHEAR = 3
WD = 1024
LANES = 128
STEPS = 2 * SHEAR + 1


def kernel(
    dims,
    basis_ref,
    fact_ref,
    shear_ref,
    window_ref,
    meas_ref,
    out_ref,
    flat,
    main_ref,
    meas_all,
    snd_halo,
    snd_meas,
    in_main,
    in_halo,
    in_meas,
    back_main,
    back_spill,
    got_main,
    got_spill,
    coef,
    sheared,
    proj,
    grad,
    spread,
    load_sem,
    send_main,
    recv_main,
    send_halo,
    recv_halo,
    send_meas,
    recv_meas,
    send_out,
    recv_out,
    send_spill,
    recv_spill,
):
    T, D, LD, HS, C, R, HL, FB, H = dims
    N = HS * C
    WIDE = C + LANES
    per = LANES // HL
    G = LD // per
    half = LD * D // 2
    me = lax.axis_index("tm")
    dep = lax.axis_index("depth")
    left = lax.rem(me + T - 1, T)
    right = lax.rem(me + 1, T)
    outward = []
    for q in range((D + 1) // 2):
        outward += [q] if q == D - 1 - q else [q, D - 1 - q]

    def peer(base, k, n):
        return lax.rem(base + k, n)

    def at(tm, depth):
        return {"tm": tm, "depth": depth}

    def remote(src, dst, send, recv, where):
        return pltpu.make_async_remote_copy(
            src_ref=src,
            dst_ref=dst,
            send_sem=send,
            recv_sem=recv,
            device_id=where,
            device_id_type=pl.DeviceIdType.MESH,
        )

    load = pltpu.make_async_copy(meas_ref, meas_all, load_sem)
    load.start()

    barrier = pltpu.get_barrier_semaphore()
    greeted = 0
    for k in range(1, T):
        pl.semaphore_signal(
            barrier, inc=1, device_id=at(peer(me, k, T), dep), device_id_type=pl.DeviceIdType.MESH
        )
        greeted += 1
    for k in range(1, D):
        for tm in (me, left, right):
            pl.semaphore_signal(
                barrier, inc=1, device_id=at(tm, peer(dep, k, D)), device_id_type=pl.DeviceIdType.MESH
            )
            greeted += 1

    count = R * LD * H
    for c in range(C // LANES):
        flat[c * count : (c + 1) * count, :] = basis_ref[:, c * LANES : (c + 1) * LANES].astype(
            jnp.float32
        )
    for c in range(C // LANES):
        for h in range(H):
            for l in range(LD):
                rows = flat[pl.ds(c * count + l * H + h, R, stride=LD * H), :]
                main_ref[
                    h // HS, h % HS, l * R : (l + 1) * R, c * LANES : (c + 1) * LANES
                ] = rows.astype(jnp.bfloat16)

    edge = lax.broadcasted_iota(jnp.int32, (R, LANES), 1)
    has_right = me < T - 1
    has_left = me > 0
    blank = jnp.zeros((R, LANES), jnp.float32)

    def pack(blocks_low, blocks_high):
        low = blank
        high = blank
        for p in range(per):
            fore = jnp.where(edge < HL, blocks_low[p], 0.0)
            aft = jnp.where(edge >= LANES - HL, blocks_high[p], 0.0)
            low = low + (pltpu.roll(fore, p * HL, 1) if p else fore)
            turn = (p * HL + HL) % LANES
            high = high + (pltpu.roll(aft, turn, 1) if turn else aft)
        return low.astype(jnp.bfloat16), high.astype(jnp.bfloat16)

    def pack_step(n, carry):
        q = n // HS
        h = n % HS
        for g in range(G):
            heads = []
            tails = []
            for p in range(per):
                rows = slice((g * per + p) * R, (g * per + p + 1) * R)
                heads.append(main_ref[q, h, rows, :LANES].astype(jnp.float32))
                tails.append(main_ref[q, h, rows, C - LANES :].astype(jnp.float32))
            low, high = pack(heads, tails)
            snd_halo[0, q, h, g * R : (g + 1) * R, :] = low
            snd_halo[1, q, h, g * R : (g + 1) * R, :] = high
        return carry

    pl.semaphore_wait(barrier, greeted)

    def main_copy(k, h):
        to = peer(dep, k, D)
        return remote(
            main_ref.at[to, h], in_main.at[dep, h], send_main.at[k, h], recv_main.at[dep, h], at(me, to)
        )

    def halo_copy(side, k, h):
        to = peer(dep, k, D)
        return remote(
            snd_halo.at[side, to, h],
            in_halo.at[side, dep, h],
            send_halo.at[side, k, h],
            recv_halo.at[side, dep, h],
            at((left, right)[side], to),
        )

    def meas_copy(k):
        to = peer(me, k, T)
        return remote(snd_meas.at[to], in_meas.at[me], send_meas.at[k], recv_meas.at[me], at(to, dep))

    for k in range(1, D):
        main_copy(k, 0).start()
    lax.fori_loop(0, D * HS, pack_step, 0)
    for h in range(HS):
        for k in list(range(1, D)) + [0]:
            if k and h:
                main_copy(k, h).start()
            for side in (0, 1):
                halo_copy(side, k, h).start()
    in_main[dep] = main_ref[dep]

    row = lax.broadcasted_iota(jnp.int32, (FB, FB), 0)
    diagonal = row == lax.broadcasted_iota(jnp.int32, (FB, FB), 1)

    def upright(values):
        spread_out = jnp.broadcast_to(values.astype(jnp.float32), (FB, FB))
        return jnp.sum(jnp.where(diagonal, spread_out, 0.0), axis=1, keepdims=True)

    low_bits = window_ref[...] & 31
    lane = lax.broadcasted_iota(jnp.int32, (FB, LANES), 1)
    pick = lax.broadcasted_iota(jnp.int32, (R, LANES), 0) == edge
    pick = jnp.where(pick, 1.0, 0.0).astype(jnp.bfloat16)
    facts = lax.dot_general(
        fact_ref[...], pick, (((0,), (0,)), ((), ())), preferred_element_type=jnp.float32
    )
    facts = jnp.where(lane == R, upright(shear_ref[...]), facts)
    facts = jnp.where(lane == R + 1, upright(window_ref[...] - low_bits), facts)
    facts = jnp.where(lane == R + 2, upright(low_bits), facts)
    facts = facts.astype(jnp.bfloat16)

    wanted = lax.broadcasted_iota(jnp.int32, (HS * FB, FB * H), 0)
    wanted = lax.rem(wanted, FB) * H + dep * HS + lax.div(wanted, FB)
    select = wanted == lax.broadcasted_iota(jnp.int32, (HS * FB, FB * H), 1)
    select = jnp.where(select, 1.0, 0.0).astype(jnp.bfloat16)
    load.wait()
    for j in range(T):
        picked = jnp.dot(
            select, meas_all[:, j * C : (j + 1) * C], preferred_element_type=jnp.float32
        ).astype(jnp.bfloat16)
        for h in range(HS):
            snd_meas[j, :, h * C : (h + 1) * C] = picked[h * FB : (h + 1) * FB, :]
        snd_meas[j, :, N:] = facts

    for k in range(1, T):
        meas_copy(k).start()
    in_meas[me] = snd_meas[me]
    for k in range(1, T):
        source = peer(me, k, T)
        remote(
            snd_meas.at[source], in_meas.at[source], send_meas.at[k], recv_meas.at[source], at(source, dep)
        ).wait_recv()

    group = (lane // R).astype(jnp.float32)

    def coef_step(j, carry):
        info = in_meas[j, :, N:].astype(jnp.float32)
        first = jnp.where(lane < R, info, 0.0)
        tiled = first
        for q in range(1, LANES // R):
            tiled = tiled + pltpu.roll(first, q * R, 1)
        step = info[:, R : R + 1] + float(SHEAR)
        rows = pl.ds(pl.multiple_of(j * FB, FB), FB)
        for b in range(2):
            coef[rows, b * LANES : (b + 1) * LANES] = jnp.where(
                step == group + float(b * (LANES // R)), tiled, 0.0
            ).astype(jnp.bfloat16)
        return carry

    lax.fori_loop(0, T, coef_step, 0)

    norm_scale = 1.0 / math.sqrt(T * FB)
    column = lax.broadcasted_iota(jnp.int32, (FB, C), 1) + me * C
    column = column.astype(jnp.float32)

    def back_copy(q, h):
        return remote(
            back_main.at[q, h], got_main.at[dep, h], send_out.at[q, h], recv_out.at[dep, h], at(me, q)
        )

    def spill_copy(side, q, h):
        return remote(
            back_spill.at[side, q, h],
            got_spill.at[side, dep, h],
            send_spill.at[side, q, h],
            recv_spill.at[side, dep, h],
            at((right, left)[side], q),
        )

    def row_step(h, carry):
        columns = pl.ds(pl.multiple_of(h * C, LANES), C)
        sheared[...] = jnp.zeros_like(sheared)
        for q in outward[::-1]:

            @pl.when(q != dep)
            def _():
                remote(
                    main_ref.at[q, h], in_main.at[q, h], send_main.at[0, h], recv_main.at[q, h], at(me, q)
                ).wait_recv()

            for side in (0, 1):
                remote(
                    snd_halo.at[side, q, h],
                    in_halo.at[side, q, h],
                    send_halo.at[side, 0, h],
                    recv_halo.at[side, q, h],
                    at((right, left)[side], q),
                ).wait_recv()
            wides = []
            for l in range(LD):
                g, p = divmod(l, per)
                body = in_main[q, h, l * R : (l + 1) * R, :].astype(jnp.float32)
                after = in_halo[0, q, h, g * R : (g + 1) * R, :].astype(jnp.float32)
                before = in_halo[1, q, h, g * R : (g + 1) * R, :].astype(jnp.float32)
                after = pltpu.roll(after, (LANES - p * HL) % LANES, 1)
                before = pltpu.roll(before, (2 * LANES - HL - p * HL) % LANES, 1)
                rim = jnp.where(
                    jnp.logical_and(edge < HL, has_right),
                    after,
                    jnp.where(jnp.logical_and(edge >= LANES - HL, has_left), before, 0.0),
                )
                wides.append(jnp.concatenate([body, rim], axis=1))
            for s in range(STEPS):
                total = sheared[s * R : (s + 1) * R, :]
                for l in range(LD):
                    shift = (s - SHEAR) * (q * LD + l - half)
                    turned = pltpu.roll(wides[l], (-shift) % WIDE, 1) if shift else wides[l]
                    total = total + turned[:, :C]
                sheared[s * R : (s + 1) * R, :] = total

        table = sheared[...]
        high = table.astype(jnp.bfloat16)
        low = (table - high.astype(jnp.float32)).astype(jnp.bfloat16)
        proj[...] = jnp.dot(coef[...], high, preferred_element_type=jnp.float32) + jnp.dot(
            coef[...], low, preferred_element_type=jnp.float32
        )

        def ray_step(j, carry):
            rows = pl.ds(pl.multiple_of(j * FB, FB), FB)
            info = in_meas[j, :, N:].astype(jnp.float32)
            start = info[:, R + 1 : R + 2] + info[:, R + 2 : R + 3]
            transmit = jnp.exp(-proj[rows, :])
            inside = jnp.logical_and(column >= start, column < start + float(WD))
            residual = jnp.where(inside, transmit - in_meas[j, :, columns].astype(jnp.float32), 0.0)
            grad[rows, :] = (-transmit * residual * norm_scale).astype(jnp.bfloat16)
            return carry

        lax.fori_loop(0, T, ray_step, 0)
        spread[...] = lax.dot_general(
            coef[...], grad[...], (((0,), (0,)), ((), ())), preferred_element_type=jnp.float32
        )

        for q in outward:
            totals = [None] * LD
            for s in range(STEPS):
                piece = jnp.concatenate([spread[s * R : (s + 1) * R, :], blank], axis=1)
                for l in range(LD):
                    shift = (s - SHEAR) * (q * LD + l - half)
                    turned = pltpu.roll(piece, shift % WIDE, 1) if shift else piece
                    totals[l] = turned if s == 0 else totals[l] + turned
            for l in range(LD):
                back_main[q, h, l * R : (l + 1) * R, :] = totals[l][:, :C].astype(jnp.bfloat16)

            @pl.when(q == dep)
            def _():
                for l in range(LD):
                    out_ref[dep * HS + h, l * R : (l + 1) * R, :] = totals[l][:, :C]

            @pl.when(q != dep)
            def _():
                back_copy(q, h).start()

            for g in range(G):
                rims = [totals[g * per + p][:, C:] for p in range(per)]
                ahead, behind = pack(rims, rims)
                back_spill[0, q, h, g * R : (g + 1) * R, :] = ahead
                back_spill[1, q, h, g * R : (g + 1) * R, :] = behind
            for side in (0, 1):
                spill_copy(side, q, h).start()
        return carry

    lax.fori_loop(0, HS, row_step, 0)

    def gather_step(h, carry):
        for k in range(D):
            source = peer(dep, k, D)
            if k:
                remote(
                    back_main.at[source, h],
                    got_main.at[source, h],
                    send_out.at[0, h],
                    recv_out.at[source, h],
                    at(me, source),
                ).wait_recv()
            for side in (0, 1):
                remote(
                    back_spill.at[side, source, h],
                    got_spill.at[side, source, h],
                    send_spill.at[side, 0, h],
                    recv_spill.at[side, source, h],
                    at((left, right)[side], source),
                ).wait_recv()
            for l in range(LD):
                g, p = divmod(l, per)
                rows = slice(l * R, (l + 1) * R)
                if k:
                    total = got_main[source, h, rows, :].astype(jnp.float32)
                else:
                    total = out_ref[source * HS + h, rows, :]
                fore = got_spill[0, source, h, g * R : (g + 1) * R, :].astype(jnp.float32)
                aft = got_spill[1, source, h, g * R : (g + 1) * R, :].astype(jnp.float32)
                fore = pltpu.roll(fore, (LANES - p * HL) % LANES, 1)
                aft = pltpu.roll(aft, (2 * LANES - HL - p * HL) % LANES, 1)
                fore = jnp.where(jnp.logical_and(edge < HL, has_left), fore, 0.0)
                aft = jnp.where(jnp.logical_and(edge >= LANES - HL, has_right), aft, 0.0)
                blocks = [total[:, b : b + LANES] for b in range(0, C, LANES)]
                blocks[0] = blocks[0] + fore
                blocks[-1] = blocks[-1] + aft
                for b, block in enumerate(blocks):
                    out_ref[source * HS + h, rows, b * LANES : (b + 1) * LANES] = block
        return carry

    lax.fori_loop(0, HS, gather_step, 0)

    for k in range(1, T):
        meas_copy(k).wait_send()

    def drain_step(h, carry):
        for k in range(D):
            if k:
                main_copy(k, h).wait_send()
            for side in (0, 1):
                halo_copy(side, k, h).wait_send()
        for q in range(D):

            @pl.when(q != dep)
            def _():
                back_copy(q, h).wait_send()

            for side in (0, 1):
                spill_copy(side, q, h).wait_send()
        return carry

    lax.fori_loop(0, HS, drain_step, 0)


def per_device(basis, factors, measured, shear, window):
    R, LD, H, C = basis.shape
    FB, W = factors.shape[0], measured.shape[2]
    T, D = lax.axis_size("tm"), lax.axis_size("depth")
    HS = H // D
    N = HS * C
    HL = 32
    while HL < SHEAR * (LD * D // 2):
        HL *= 2
    G = LD // (LANES // HL)

    bf, f32 = jnp.bfloat16, jnp.float32
    dma = pltpu.SemaphoreType.DMA
    whole = pl.BlockSpec(memory_space=pltpu.VMEM)
    out = pl.pallas_call(
        functools.partial(kernel, (T, D, LD, HS, C, R, HL, FB, H)),
        out_shape=jax.ShapeDtypeStruct((H, LD * R, C), f32),
        in_specs=[whole, whole, whole, whole, pl.BlockSpec(memory_space=pl.ANY)],
        out_specs=whole,
        scratch_shapes=[
            pltpu.VMEM((C // LANES * R * LD * H, LANES), f32),
            pltpu.VMEM((D, HS, LD * R, C), bf),
            pltpu.VMEM((FB * H, W), bf),
            pltpu.VMEM((2, D, HS, G * R, LANES), bf),
            pltpu.VMEM((T, FB, N + LANES), bf),
            pltpu.VMEM((D, HS, LD * R, C), bf),
            pltpu.VMEM((2, D, HS, G * R, LANES), bf),
            pltpu.VMEM((T, FB, N + LANES), bf),
            pltpu.VMEM((D, HS, LD * R, C), bf),
            pltpu.VMEM((2, D, HS, G * R, LANES), bf),
            pltpu.VMEM((D, HS, LD * R, C), bf),
            pltpu.VMEM((2, D, HS, G * R, LANES), bf),
            pltpu.VMEM((T * FB, 2 * LANES), bf),
            pltpu.VMEM((2 * LANES, C), f32),
            pltpu.VMEM((T * FB, C), f32),
            pltpu.VMEM((T * FB, C), bf),
            pltpu.VMEM((2 * LANES, C), f32),
            dma,
            dma((D, HS)),
            dma((D, HS)),
            dma((2, D, HS)),
            dma((2, D, HS)),
            dma((T,)),
            dma((T,)),
            dma((D, HS)),
            dma((D, HS)),
            dma((2, D, HS)),
            dma((2, D, HS)),
        ],
        compiler_params=pltpu.CompilerParams(
            collective_id=0, has_side_effects=True, vmem_limit_bytes=60 * 1024 * 1024
        ),
    )(basis.reshape(R * LD * H, C), factors.T, shear.reshape(1, FB), window.reshape(1, FB), measured.reshape(FB * H, W))
    return jnp.transpose(out.reshape(H, LD, R, C), (2, 1, 0, 3))


def solution(mesh):
    in_specs = (P(None, "depth", None, "tm"), P("tm", None), P("tm", None, None), P("tm"), P("tm"))
    out_specs = P(None, "depth", None, "tm")
    return jax.shard_map(
        per_device, mesh=mesh, in_specs=in_specs, out_specs=out_specs, check_vma=False
    )
```

```python
import functools
import math

import jax
import jax.numpy as jnp
from jax import lax
from jax.experimental import pallas as pl
from jax.experimental.pallas import tpu as pltpu
from jax.sharding import PartitionSpec as P

SHEAR = 3
WD = 1024
LANES = 128
STEPS = 2 * SHEAR + 1


def kernel(
    dims,
    basis_ref,
    fact_ref,
    shear_ref,
    window_ref,
    meas_ref,
    out_ref,
    own,
    placed,
    flat,
    main_ref,
    meas_all,
    snd_halo,
    snd_meas,
    in_main,
    in_halo,
    in_meas,
    back_main,
    back_spill,
    got_main,
    got_spill,
    coef,
    sheared,
    proj,
    grad,
    spread,
    load_sem,
    send_main,
    recv_main,
    send_halo,
    recv_halo,
    send_meas,
    recv_meas,
    send_out,
    recv_out,
    send_spill,
    recv_spill,
):
    T, D, LD, HS, C, R, HL, FB, H = dims
    N = HS * C
    WIDE = C + LANES
    per = LANES // HL
    G = LD // per
    half = LD * D // 2
    me = lax.axis_index("tm")
    dep = lax.axis_index("depth")
    left = lax.rem(me + T - 1, T)
    right = lax.rem(me + 1, T)
    outward = []
    for q in range((D + 1) // 2):
        outward += [q] if q == D - 1 - q else [q, D - 1 - q]

    def peer(base, k, n):
        return lax.rem(base + k, n)

    def at(tm, depth):
        return {"tm": tm, "depth": depth}

    def remote(src, dst, send, recv, where):
        return pltpu.make_async_remote_copy(
            src_ref=src,
            dst_ref=dst,
            send_sem=send,
            recv_sem=recv,
            device_id=where,
            device_id_type=pl.DeviceIdType.MESH,
        )

    load = pltpu.make_async_copy(meas_ref, meas_all, load_sem)
    load.start()

    barrier = pltpu.get_barrier_semaphore()
    greeted = 0
    for k in range(1, T):
        pl.semaphore_signal(
            barrier, inc=1, device_id=at(peer(me, k, T), dep), device_id_type=pl.DeviceIdType.MESH
        )
        greeted += 1
    for k in range(1, D):
        for tm in (me, left, right):
            pl.semaphore_signal(
                barrier, inc=1, device_id=at(tm, peer(dep, k, D)), device_id_type=pl.DeviceIdType.MESH
            )
            greeted += 1

    count = R * LD * H
    for c in range(C // LANES):
        flat[c * count : (c + 1) * count, :] = basis_ref[:, c * LANES : (c + 1) * LANES].astype(
            jnp.float32
        )
    for c in range(C // LANES):
        for h in range(H):
            for l in range(LD):
                rows = flat[pl.ds(c * count + l * H + h, R, stride=LD * H), :]
                main_ref[
                    h // HS, h % HS, l * R : (l + 1) * R, c * LANES : (c + 1) * LANES
                ] = rows.astype(jnp.bfloat16)

    edge = lax.broadcasted_iota(jnp.int32, (R, LANES), 1)
    has_right = me < T - 1
    has_left = me > 0
    blank = jnp.zeros((R, LANES), jnp.float32)

    def pack(blocks_low, blocks_high):
        low = blank
        high = blank
        for p in range(per):
            fore = jnp.where(edge < HL, blocks_low[p], 0.0)
            aft = jnp.where(edge >= LANES - HL, blocks_high[p], 0.0)
            low = low + (pltpu.roll(fore, p * HL, 1) if p else fore)
            turn = (p * HL + HL) % LANES
            high = high + (pltpu.roll(aft, turn, 1) if turn else aft)
        return low.astype(jnp.bfloat16), high.astype(jnp.bfloat16)

    def pack_step(n, carry):
        q = n // HS
        h = n % HS
        for g in range(G):
            heads = []
            tails = []
            for p in range(per):
                rows = slice((g * per + p) * R, (g * per + p + 1) * R)
                heads.append(main_ref[q, h, rows, :LANES].astype(jnp.float32))
                tails.append(main_ref[q, h, rows, C - LANES :].astype(jnp.float32))
            low, high = pack(heads, tails)
            snd_halo[0, q, h, g * R : (g + 1) * R, :] = low
            snd_halo[1, q, h, g * R : (g + 1) * R, :] = high
        return carry

    pl.semaphore_wait(barrier, greeted)

    def main_copy(k, h):
        to = peer(dep, k, D)
        return remote(
            main_ref.at[to, h], in_main.at[dep, h], send_main.at[k, h], recv_main.at[dep, h], at(me, to)
        )

    def halo_copy(side, k, h):
        to = peer(dep, k, D)
        return remote(
            snd_halo.at[side, to, h],
            in_halo.at[side, dep, h],
            send_halo.at[side, k, h],
            recv_halo.at[side, dep, h],
            at((left, right)[side], to),
        )

    def meas_copy(k):
        to = peer(me, k, T)
        return remote(snd_meas.at[to], in_meas.at[me], send_meas.at[k], recv_meas.at[me], at(to, dep))

    for k in range(1, D):
        main_copy(k, 0).start()
    lax.fori_loop(0, D * HS, pack_step, 0)
    for h in range(HS):
        for k in list(range(1, D)) + [0]:
            if k and h:
                main_copy(k, h).start()
            for side in (0, 1):
                halo_copy(side, k, h).start()
    in_main[dep] = main_ref[dep]

    row = lax.broadcasted_iota(jnp.int32, (FB, FB), 0)
    diagonal = row == lax.broadcasted_iota(jnp.int32, (FB, FB), 1)

    def upright(values):
        spread_out = jnp.broadcast_to(values.astype(jnp.float32), (FB, FB))
        return jnp.sum(jnp.where(diagonal, spread_out, 0.0), axis=1, keepdims=True)

    low_bits = window_ref[...] & 31
    lane = lax.broadcasted_iota(jnp.int32, (FB, LANES), 1)
    pick = lax.broadcasted_iota(jnp.int32, (R, LANES), 0) == edge
    pick = jnp.where(pick, 1.0, 0.0).astype(jnp.bfloat16)
    facts = lax.dot_general(
        fact_ref[...], pick, (((0,), (0,)), ((), ())), preferred_element_type=jnp.float32
    )
    facts = jnp.where(lane == R, upright(shear_ref[...]), facts)
    facts = jnp.where(lane == R + 1, upright(window_ref[...] - low_bits), facts)
    facts = jnp.where(lane == R + 2, upright(low_bits), facts)
    facts = facts.astype(jnp.bfloat16)

    wanted = lax.broadcasted_iota(jnp.int32, (HS * FB, FB * H), 0)
    wanted = lax.rem(wanted, FB) * H + dep * HS + lax.div(wanted, FB)
    select = wanted == lax.broadcasted_iota(jnp.int32, (HS * FB, FB * H), 1)
    select = jnp.where(select, 1.0, 0.0).astype(jnp.bfloat16)
    load.wait()
    for j in range(T):
        picked = jnp.dot(
            select, meas_all[:, j * C : (j + 1) * C], preferred_element_type=jnp.float32
        ).astype(jnp.bfloat16)
        for h in range(HS):
            snd_meas[j, :, h * C : (h + 1) * C] = picked[h * FB : (h + 1) * FB, :]
        snd_meas[j, :, N:] = facts

    for k in range(1, T):
        meas_copy(k).start()
    in_meas[me] = snd_meas[me]
    for k in range(1, T):
        source = peer(me, k, T)
        remote(
            snd_meas.at[source], in_meas.at[source], send_meas.at[k], recv_meas.at[source], at(source, dep)
        ).wait_recv()

    group = (lane // R).astype(jnp.float32)

    def coef_step(j, carry):
        info = in_meas[j, :, N:].astype(jnp.float32)
        first = jnp.where(lane < R, info, 0.0)
        tiled = first
        for q in range(1, LANES // R):
            tiled = tiled + pltpu.roll(first, q * R, 1)
        step = info[:, R : R + 1] + float(SHEAR)
        rows = pl.ds(pl.multiple_of(j * FB, FB), FB)
        for b in range(2):
            coef[rows, b * LANES : (b + 1) * LANES] = jnp.where(
                step == group + float(b * (LANES // R)), tiled, 0.0
            ).astype(jnp.bfloat16)
        return carry

    lax.fori_loop(0, T, coef_step, 0)

    norm_scale = 1.0 / math.sqrt(T * FB)
    column = lax.broadcasted_iota(jnp.int32, (FB, C), 1) + me * C
    column = column.astype(jnp.float32)

    def back_copy(q, h):
        return remote(
            back_main.at[q, h], got_main.at[dep, h], send_out.at[q, h], recv_out.at[dep, h], at(me, q)
        )

    def spill_copy(side, q, h):
        return remote(
            back_spill.at[side, q, h],
            got_spill.at[side, dep, h],
            send_spill.at[side, q, h],
            recv_spill.at[side, dep, h],
            at((right, left)[side], q),
        )

    def row_step(h, carry):
        columns = pl.ds(pl.multiple_of(h * C, LANES), C)
        sheared[...] = jnp.zeros_like(sheared)
        for q in outward[::-1]:

            @pl.when(q != dep)
            def _():
                remote(
                    main_ref.at[q, h], in_main.at[q, h], send_main.at[0, h], recv_main.at[q, h], at(me, q)
                ).wait_recv()

            for side in (0, 1):
                remote(
                    snd_halo.at[side, q, h],
                    in_halo.at[side, q, h],
                    send_halo.at[side, 0, h],
                    recv_halo.at[side, q, h],
                    at((right, left)[side], q),
                ).wait_recv()
            wides = []
            for l in range(LD):
                g, p = divmod(l, per)
                body = in_main[q, h, l * R : (l + 1) * R, :].astype(jnp.float32)
                after = in_halo[0, q, h, g * R : (g + 1) * R, :].astype(jnp.float32)
                before = in_halo[1, q, h, g * R : (g + 1) * R, :].astype(jnp.float32)
                after = pltpu.roll(after, (LANES - p * HL) % LANES, 1)
                before = pltpu.roll(before, (2 * LANES - HL - p * HL) % LANES, 1)
                rim = jnp.where(
                    jnp.logical_and(edge < HL, has_right),
                    after,
                    jnp.where(jnp.logical_and(edge >= LANES - HL, has_left), before, 0.0),
                )
                wides.append(jnp.concatenate([body, rim], axis=1))
            for s in range(STEPS):
                total = sheared[s * R : (s + 1) * R, :]
                for l in range(LD):
                    shift = (s - SHEAR) * (q * LD + l - half)
                    turned = pltpu.roll(wides[l], (-shift) % WIDE, 1) if shift else wides[l]
                    total = total + turned[:, :C]
                sheared[s * R : (s + 1) * R, :] = total

        table = sheared[...]
        high = table.astype(jnp.bfloat16)
        low = (table - high.astype(jnp.float32)).astype(jnp.bfloat16)
        proj[...] = jnp.dot(coef[...], high, preferred_element_type=jnp.float32) + jnp.dot(
            coef[...], low, preferred_element_type=jnp.float32
        )

        def ray_step(j, carry):
            rows = pl.ds(pl.multiple_of(j * FB, FB), FB)
            info = in_meas[j, :, N:].astype(jnp.float32)
            start = info[:, R + 1 : R + 2] + info[:, R + 2 : R + 3]
            transmit = jnp.exp(-proj[rows, :])
            inside = jnp.logical_and(column >= start, column < start + float(WD))
            residual = jnp.where(inside, transmit - in_meas[j, :, columns].astype(jnp.float32), 0.0)
            grad[rows, :] = (-transmit * residual * norm_scale).astype(jnp.bfloat16)
            return carry

        lax.fori_loop(0, T, ray_step, 0)
        spread[...] = lax.dot_general(
            coef[...], grad[...], (((0,), (0,)), ((), ())), preferred_element_type=jnp.float32
        )

        for q in outward:
            totals = [None] * LD
            for s in range(STEPS):
                piece = jnp.concatenate([spread[s * R : (s + 1) * R, :], blank], axis=1)
                for l in range(LD):
                    shift = (s - SHEAR) * (q * LD + l - half)
                    turned = pltpu.roll(piece, shift % WIDE, 1) if shift else piece
                    totals[l] = turned if s == 0 else totals[l] + turned
            for l in range(LD):
                back_main[q, h, l * R : (l + 1) * R, :] = totals[l][:, :C].astype(jnp.bfloat16)

            @pl.when(q == dep)
            def _():
                for l in range(LD):
                    own[h, l * R : (l + 1) * R, :] = totals[l][:, :C]

            @pl.when(q != dep)
            def _():
                back_copy(q, h).start()

            for g in range(G):
                rims = [totals[g * per + p][:, C:] for p in range(per)]
                ahead, behind = pack(rims, rims)
                back_spill[0, q, h, g * R : (g + 1) * R, :] = ahead
                back_spill[1, q, h, g * R : (g + 1) * R, :] = behind
            for side in (0, 1):
                spill_copy(side, q, h).start()
        return carry

    lax.fori_loop(0, HS, row_step, 0)

    def gather_step(h, carry):
        for k in range(D):
            source = peer(dep, k, D)
            if k:
                remote(
                    back_main.at[source, h],
                    got_main.at[source, h],
                    send_out.at[0, h],
                    recv_out.at[source, h],
                    at(me, source),
                ).wait_recv()
            for side in (0, 1):
                remote(
                    back_spill.at[side, source, h],
                    got_spill.at[side, source, h],
                    send_spill.at[side, 0, h],
                    recv_spill.at[side, source, h],
                    at((left, right)[side], source),
                ).wait_recv()
            for l in range(LD):
                g, p = divmod(l, per)
                rows = slice(l * R, (l + 1) * R)
                if k:
                    total = got_main[source, h, rows, :].astype(jnp.float32)
                else:
                    total = own[h, rows, :]
                fore = got_spill[0, source, h, g * R : (g + 1) * R, :].astype(jnp.float32)
                aft = got_spill[1, source, h, g * R : (g + 1) * R, :].astype(jnp.float32)
                fore = pltpu.roll(fore, (LANES - p * HL) % LANES, 1)
                aft = pltpu.roll(aft, (2 * LANES - HL - p * HL) % LANES, 1)
                fore = jnp.where(jnp.logical_and(edge < HL, has_left), fore, 0.0)
                aft = jnp.where(jnp.logical_and(edge >= LANES - HL, has_right), aft, 0.0)
                blocks = [total[:, b : b + LANES] for b in range(0, C, LANES)]
                blocks[0] = blocks[0] + fore
                blocks[-1] = blocks[-1] + aft
                for b, block in enumerate(blocks):
                    first = b * count + l * H + source * HS + h
                    placed[pl.ds(first, R, stride=LD * H), :] = block
        return carry

    lax.fori_loop(0, HS, gather_step, 0)
    for c in range(C // LANES):
        out_ref[:, c * LANES : (c + 1) * LANES] = placed[c * count : (c + 1) * count, :]

    for k in range(1, T):
        meas_copy(k).wait_send()

    def drain_step(h, carry):
        for k in range(D):
            if k:
                main_copy(k, h).wait_send()
            for side in (0, 1):
                halo_copy(side, k, h).wait_send()
        for q in range(D):

            @pl.when(q != dep)
            def _():
                back_copy(q, h).wait_send()

            for side in (0, 1):
                spill_copy(side, q, h).wait_send()
        return carry

    lax.fori_loop(0, HS, drain_step, 0)


def per_device(basis, factors, measured, shear, window):
    R, LD, H, C = basis.shape
    FB, W = factors.shape[0], measured.shape[2]
    T, D = lax.axis_size("tm"), lax.axis_size("depth")
    HS = H // D
    N = HS * C
    HL = 32
    while HL < SHEAR * (LD * D // 2):
        HL *= 2
    G = LD // (LANES // HL)

    bf, f32 = jnp.bfloat16, jnp.float32
    dma = pltpu.SemaphoreType.DMA
    whole = pl.BlockSpec(memory_space=pltpu.VMEM)
    out = pl.pallas_call(
        functools.partial(kernel, (T, D, LD, HS, C, R, HL, FB, H)),
        out_shape=jax.ShapeDtypeStruct((R * LD * H, C), f32),
        in_specs=[whole, whole, whole, whole, pl.BlockSpec(memory_space=pl.ANY)],
        out_specs=whole,
        scratch_shapes=[
            pltpu.VMEM((HS, LD * R, C), f32),
            pltpu.VMEM((C // LANES * R * LD * H, LANES), f32),
            pltpu.VMEM((C // LANES * R * LD * H, LANES), f32),
            pltpu.VMEM((D, HS, LD * R, C), bf),
            pltpu.VMEM((FB * H, W), bf),
            pltpu.VMEM((2, D, HS, G * R, LANES), bf),
            pltpu.VMEM((T, FB, N + LANES), bf),
            pltpu.VMEM((D, HS, LD * R, C), bf),
            pltpu.VMEM((2, D, HS, G * R, LANES), bf),
            pltpu.VMEM((T, FB, N + LANES), bf),
            pltpu.VMEM((D, HS, LD * R, C), bf),
            pltpu.VMEM((2, D, HS, G * R, LANES), bf),
            pltpu.VMEM((D, HS, LD * R, C), bf),
            pltpu.VMEM((2, D, HS, G * R, LANES), bf),
            pltpu.VMEM((T * FB, 2 * LANES), bf),
            pltpu.VMEM((2 * LANES, C), f32),
            pltpu.VMEM((T * FB, C), f32),
            pltpu.VMEM((T * FB, C), bf),
            pltpu.VMEM((2 * LANES, C), f32),
            dma,
            dma((D, HS)),
            dma((D, HS)),
            dma((2, D, HS)),
            dma((2, D, HS)),
            dma((T,)),
            dma((T,)),
            dma((D, HS)),
            dma((D, HS)),
            dma((2, D, HS)),
            dma((2, D, HS)),
        ],
        compiler_params=pltpu.CompilerParams(
            collective_id=0, has_side_effects=True, vmem_limit_bytes=60 * 1024 * 1024
        ),
    )(basis.reshape(R * LD * H, C), factors.T, shear.reshape(1, FB), window.reshape(1, FB), measured.reshape(FB * H, W))
    return out.reshape(R, LD, H, C)


def solution(mesh):
    in_specs = (P(None, "depth", None, "tm"), P("tm", None), P("tm", None, None), P("tm"), P("tm"))
    out_specs = P(None, "depth", None, "tm")
    return jax.shard_map(
        per_device, mesh=mesh, in_specs=in_specs, out_specs=out_specs, check_vma=False
    )
```
